128 devices in a mesh: tok: 32 (over z, y_lo, x), head: 4 (over y_hi, core).
Axes of the slice: x: 4, y: 4 (y_hi: 2, y_lo: 2; y = y_hi * 2 + y_lo), z: 4, core: 2. Of those that a mesh axis runs over, the one named last changes fastest.
Arguments:
- queries: bfloat16 [32768, 8192], P('tok', 'head'), may hold values from -12 to 12
- keys: bfloat16 [32768, 1024], P('tok', 'head'), may hold values from -12 to 12
- values: bfloat16 [32768, 1024], P('tok', 'head'), may hold values from -6 to 6
- tile_docs: int32 [256], P('tok'), may hold values from 0 to 255, as said below
Outputs:
- attention: bfloat16 [32768, 8192], P(('tok', 'head'))
The draws below stay inside these ranges and needn't reach their ends.
Inputs may be any that keep to these rules, and one draw needn't show every extreme that they name: `tile_docs`: each tile holds the index of the first tile of its document, so numbers never fall and are equal exactly within a document; tile 0 and the last tile each begin a document; every block of 8 tiles along tok holds the first tile of some document after its own first tile, so that a document lies within the blocks of at most two neighbouring indices of tok. The block of an even index of tok begins with a document; the block of an odd index never does, so its first document reaches back into the previous block.
All inputs are finite; a program needn't handle non-finite values.
Results may differ from the reference program's by a relative error of at most 0.004.
Values may be sent and summed in bfloat16 or wider, within the bound.
A program may use at most 128 MiB of HBM per device.

```python
import jax
import jax.numpy as jnp
from jax import lax

HEAD_DIM = 128
QPK = 8
KV_HEADS = 8
TILE = 128
TOK_DEV = 1024
TOKENS = 32768
TILES = 256
TILES_DEV = 8
N_TOK = 32


def draw_queries(key, part):
    base_key = jax.random.fold_in(key, 1)
    drawn = jax.random.truncated_normal(base_key, -6.0, 6.0, (TOKENS, KV_HEADS, QPK, HEAD_DIM), jnp.float32)
    return drawn.reshape(TOKENS, KV_HEADS * QPK * HEAD_DIM).astype(jnp.bfloat16)


def draw_keys(key, part):
    base_key = jax.random.fold_in(key, 2)
    drawn = jax.random.truncated_normal(base_key, -6.0, 6.0, (TOKENS, KV_HEADS, HEAD_DIM), jnp.float32)
    return drawn.reshape(TOKENS, KV_HEADS * HEAD_DIM).astype(jnp.bfloat16)


def draw_tile_docs(key, part):
    devices = TILES // TILES_DEV
    inner_starts = jax.random.randint(jax.random.fold_in(key, 11), (devices, TILES_DEV), 0, 3) == 0
    forced = jax.random.randint(jax.random.fold_in(key, 12), (devices, 1), 1, TILES_DEV)
    columns = jnp.arange(TILES_DEV)[None, :]
    starts = inner_starts | (columns == forced)
    even_device = jnp.arange(devices)[:, None] % 2 == 0
    starts = jnp.where(columns == 0, even_device, starts)
    flat_starts = starts.reshape(-1)
    tile_index = jnp.arange(TILES, dtype=jnp.int32)
    flat_starts = flat_starts | (tile_index == 0) | (tile_index == TILES - 1)
    marked = jnp.where(flat_starts, tile_index, jnp.int32(0)).astype(jnp.int32)
    return lax.cummax(marked, axis=0).astype(jnp.int32)


def block_scale(own_key, extent, pieces, low, high):
    def one(axis_at, shards_of):
        draws = jax.random.uniform(jax.random.fold_in(jax.random.fold_in(own_key, 6), axis_at), (shards_of,), jnp.float32, low / len(pieces), high / len(pieces))
        return jnp.repeat(jnp.exp(draws), extent[axis_at] // shards_of).reshape((-1,) + (1,) * (len(extent) - axis_at - 1))

    level = one(*pieces[0])
    for cut in pieces[1:]:
        level = level * one(*cut)
    return level


def centred(stream_key, dims, width, reach, pieces=(), kind=jnp.bfloat16):
    factor_of = block_scale(stream_key, dims, pieces, -0.22, 0.18) if pieces else 1.0
    values = jax.random.normal(stream_key, dims, jnp.float32) * width * factor_of
    return jnp.minimum(jnp.maximum(values, -reach), reach).astype(kind)


def setup_inputs(seed: int = 0) -> dict:
    seeds = jax.random.split(jax.random.key(seed), 5)
    queries = draw_queries(jax.random.fold_in(seeds[4], 71), 0)
    keys = draw_keys(jax.random.fold_in(seeds[4], 71), 0)
    values = centred(seeds[2], (TOKENS, KV_HEADS * HEAD_DIM), 1.0, 6.0, ((0, 32), (1, 4)))
    tile_docs = draw_tile_docs(jax.random.fold_in(seeds[4], 71), 0)
    return dict(queries=queries, keys=keys, values=values, tile_docs=tile_docs)


def reference(queries, keys, values, tile_docs):
    row_docs = jnp.repeat(tile_docs, TILE)
    score_scale = HEAD_DIM ** -0.5
    row_width = KV_HEADS * QPK * HEAD_DIM

    def one_block(block_index):
        first_row = block_index * TOK_DEV
        earlier_row = jnp.maximum(block_index - 1, 0) * TOK_DEV
        query_rows = lax.dynamic_slice_in_dim(queries, first_row, TOK_DEV, 0).astype(jnp.float32)
        query_rows = query_rows.reshape(TOK_DEV, KV_HEADS, QPK, HEAD_DIM)
        key_rows = jnp.concatenate([lax.dynamic_slice_in_dim(keys, earlier_row, TOK_DEV, 0), lax.dynamic_slice_in_dim(keys, first_row, TOK_DEV, 0)], 0)
        key_rows = key_rows.astype(jnp.float32).reshape(2 * TOK_DEV, KV_HEADS, HEAD_DIM)
        value_rows = jnp.concatenate([lax.dynamic_slice_in_dim(values, earlier_row, TOK_DEV, 0), lax.dynamic_slice_in_dim(values, first_row, TOK_DEV, 0)], 0)
        value_rows = value_rows.astype(jnp.float32).reshape(2 * TOK_DEV, KV_HEADS, HEAD_DIM)
        earlier_docs = jnp.where(block_index == 0, jnp.int32(-1), lax.dynamic_slice_in_dim(row_docs, earlier_row, TOK_DEV, 0))
        query_docs = lax.dynamic_slice_in_dim(row_docs, first_row, TOK_DEV, 0)
        key_docs = jnp.concatenate([earlier_docs, query_docs], 0)
        causal = jnp.arange(2 * TOK_DEV)[None, :] <= (jnp.arange(TOK_DEV) + TOK_DEV)[:, None]
        visible = (query_docs[:, None] == key_docs[None, :]) & causal
        scores = jnp.einsum("qgha,kga->ghqk", query_rows, key_rows) * score_scale
        scores = jnp.where(visible, scores, -1e30)
        maxima = jnp.max(scores, axis=-1, keepdims=True)
        weights = jnp.where(visible, jnp.exp(scores - maxima), 0.0)
        totals = jnp.sum(weights, axis=-1)
        rounded = lax.optimization_barrier(weights.astype(jnp.bfloat16)).astype(jnp.float32)
        summed = jnp.einsum("ghqk,kga->ghqa", rounded, value_rows) / totals[..., None]
        return jnp.transpose(summed, (2, 0, 1, 3)).reshape(TOK_DEV, row_width).astype(jnp.bfloat16)

    blocks = lax.map(one_block, jnp.arange(N_TOK, dtype=jnp.int32))
    return blocks.reshape(TOKENS, row_width)
```

```python
import functools

import jax
import jax.numpy as jnp
from jax import lax
from jax.experimental import pallas as pl
from jax.experimental.pallas import tpu as pltpu
from jax.sharding import PartitionSpec as P

HEAD_DIM = 128
QPK = 8
TILE = 128
MESH = pl.DeviceIdType.MESH
HIDDEN = -1e30
EXPONENT_SCALE = HEAD_DIM**-0.5 * 1.4426950408889634
STACK = 2
CHUNK = 256


def kernel(docs, q_hbm, k_hbm, v_hbm, out, q, keys, vals, bias, stage,
           q_sem, kv_sem, rim_send, rim_recv, send_sem, recv_sem, own_sem):
    tok, head = lax.axis_index("tok"), lax.axis_index("head")
    y_hi, core = head // 2, head % 2
    odd = tok % 2
    sibling = (tok, 2 * y_hi + 1 - core)
    across = [(tok, 2 * (1 - y_hi) + c) for c in range(2)]
    neighbour = (tok + 1 - 2 * odd, head)

    barrier = pltpu.get_barrier_semaphore()
    for device in (sibling, *across, neighbour):
        pl.semaphore_signal(barrier, inc=1, device_id=device, device_id_type=MESH)

    far, near = 4 * (1 - y_hi), 4 * y_hi

    def load_q(part):
        first = pl.multiple_of(jnp.where(part == 0, far, near) * TILE, 4 * TILE)
        rows = pl.ds(first, 4 * TILE)
        return pltpu.make_async_copy(q_hbm.at[rows], q.at[rows], q_sem.at[part])

    def load_kv(g):
        source = (slice(None), pl.ds(g * HEAD_DIM, HEAD_DIM))
        target = (g, pl.ds(7 * TILE, 8 * TILE))
        return (
            pltpu.make_async_copy(k_hbm.at[source], keys.at[target], kv_sem.at[0, g]),
            pltpu.make_async_copy(v_hbm.at[source], vals.at[target], kv_sem.at[1, g]),
        )

    def rim(g):
        source = (pl.ds(TILE, 7 * TILE), pl.ds(g * HEAD_DIM, HEAD_DIM))
        target = (g, pl.ds(0, 7 * TILE))
        return [
            pltpu.make_async_remote_copy(
                src_ref=here.at[source], dst_ref=there.at[target],
                send_sem=rim_send.at[which, g], recv_sem=rim_recv.at[which, g],
                device_id=neighbour, device_id_type=MESH,
            )
            for which, (here, there) in enumerate(((k_hbm, keys), (v_hbm, vals)))
        ]

    for copy in load_kv(0):
        copy.start()
    load_q(0).start()
    for copy in load_kv(1):
        copy.start()
    load_q(1).start()

    blank = jnp.zeros((TILE, HEAD_DIM), jnp.bfloat16)
    for g in range(2):
        keys[g, 15 * TILE :] = blank
        vals[g, 15 * TILE :] = blank

    @pl.when(odd == 0)
    def _():
        for g in range(2):
            keys[g, 6 * TILE : 7 * TILE] = blank
            vals[g, 6 * TILE : 7 * TILE] = blank

    pl.semaphore_wait(barrier, 4)

    @pl.when(odd == 0)
    def _():
        for g in range(2):
            for copy in rim(g):
                copy.start()

    eye = (
        lax.broadcasted_iota(jnp.int32, (TILE, TILE), 0)
        == lax.broadcasted_iota(jnp.int32, (TILE, TILE), 1)
    ).astype(jnp.float32).astype(jnp.bfloat16)

    def attend(i, g, t, first, chunks):
        length = chunks * CHUNK
        span = pl.ds(pl.multiple_of(first * CHUNK, CHUNK), length)
        rows = pl.ds(pl.multiple_of(t * TILE, TILE), TILE)

        def group(j, carry):
            base = pl.multiple_of((g * QPK + j * STACK) * HEAD_DIM, STACK * HEAD_DIM)
            wide = q[rows, pl.ds(base, STACK * HEAD_DIM)]
            queries = jnp.concatenate(
                [
                    jnp.concatenate([wide[:, a * HEAD_DIM : (a + 1) * HEAD_DIM], eye], 1)
                    for a in range(STACK)
                ],
                0,
            )
            known = jnp.concatenate([keys[g, span], bias[span]], 1)
            scores = lax.dot_general(
                queries, known, (((1,), (1,)), ((), ())), preferred_element_type=jnp.float32
            )
            maxima = jnp.max(scores, axis=1, keepdims=True)
            weights = jnp.exp2((scores - maxima) * EXPONENT_SCALE).astype(jnp.bfloat16)
            summed = jnp.dot(
                weights,
                jnp.concatenate(
                    [vals[g, span], jnp.ones((length, HEAD_DIM), jnp.bfloat16)], 1
                ),
                preferred_element_type=jnp.float32,
            )
            result = (summed[:, :HEAD_DIM] / summed[:, HEAD_DIM:]).astype(jnp.bfloat16)
            stage[i, :, pl.ds(pl.multiple_of(j * STACK * HEAD_DIM, STACK * HEAD_DIM), STACK * HEAD_DIM)] = (
                jnp.concatenate([result[a * TILE : (a + 1) * TILE] for a in range(STACK)], 1)
            )
            return carry

        lax.fori_loop(0, QPK // STACK, group, 0)

    def place(i):
        crossing = i < 8
        g = jnp.where(crossing, i // 4, (i // 2) % 2)
        t = jnp.where(
            crossing, far + i % 4, near + 2 * jnp.where(i < 12, 1 - core, core) + i % 2
        )
        return g, t

    def send(i):
        g, t = place(i)
        return pltpu.make_async_remote_copy(
            src_ref=stage.at[i],
            dst_ref=out.at[
                pl.ds(pl.multiple_of((t % 2) * TILE, TILE), TILE),
                pl.ds(pl.multiple_of((head * 2 + g) * QPK * HEAD_DIM, QPK * HEAD_DIM), QPK * HEAD_DIM),
            ],
            send_sem=send_sem.at[i],
            recv_sem=recv_sem.at[head, g, t % 2],
            device_id=(tok, t // 2),
            device_id_type=MESH,
        )

    def keep(i):
        g, t = place(i)
        return pltpu.make_async_copy(
            stage.at[i],
            out.at[
                pl.ds(pl.multiple_of((t % 2) * TILE, TILE), TILE),
                pl.ds(pl.multiple_of((head * 2 + g) * QPK * HEAD_DIM, QPK * HEAD_DIM), QPK * HEAD_DIM),
            ],
            own_sem.at[i - 12],
        )

    def unit(i, carry):
        g, t = place(i)

        @pl.when(i % 4 == 0)
        def _():
            @pl.when(i < 8)
            def _():
                for copy in load_kv(i // 4):
                    copy.wait()

                @pl.when(odd == 1)
                def _():
                    for copy in rim(i // 4):
                        copy.wait_recv()

            @pl.when(i == 0)
            def _():
                load_q(0).wait()

            @pl.when(i == 8)
            def _():
                load_q(1).wait()

        reaches_back = jnp.where(t == 7, 0, odd)
        first = 3 - 3 * reaches_back
        count = (7 + t) // 2 + 1 - first
        begin = (docs[t] - 8 * tok + 7) * TILE
        row = lax.broadcasted_iota(jnp.int32, (CHUNK, TILE), 1) + (7 + t) * TILE

        def hide(c, carry):
            at = pl.multiple_of((first + c) * CHUNK, CHUNK)
            key = lax.broadcasted_iota(jnp.int32, (CHUNK, TILE), 0) + at
            bias[pl.ds(at, CHUNK)] = jnp.where(
                (key >= begin) & (key <= row), 0.0, HIDDEN
            ).astype(jnp.bfloat16)
            return carry

        lax.fori_loop(0, count, hide, 0)

        for chunks in range(1, 8):
            @pl.when(count == chunks)
            def _(chunks=chunks):
                attend(i, g, t, first, chunks)

        @pl.when(i < 12)
        def _():
            send(i).start()

        @pl.when(i >= 12)
        def _():
            keep(i).start()

        return carry

    lax.fori_loop(0, 16, unit, 0)

    @pl.when(odd == 0)
    def _():
        for g in range(2):
            for copy in rim(g):
                copy.wait_send()

    def finish(i, carry):
        send(i).wait_send()
        return carry

    lax.fori_loop(0, 12, finish, 0)
    for i in range(12, 16):
        keep(i).wait()

    def arrive(n, carry):
        other = (head + 1 + n // 4) % 4
        g, half = (n // 2) % 2, n % 2
        piece = out.at[
            pl.ds(pl.multiple_of(half * TILE, TILE), TILE),
            pl.ds(pl.multiple_of((other * 2 + g) * QPK * HEAD_DIM, QPK * HEAD_DIM), QPK * HEAD_DIM),
        ]
        pltpu.make_async_remote_copy(
            src_ref=stage.at[0], dst_ref=piece, send_sem=send_sem.at[0],
            recv_sem=recv_sem.at[other, g, half], device_id=sibling, device_id_type=MESH,
        ).wait_recv()
        return carry

    lax.fori_loop(0, 12, arrive, 0)


def local(queries, keys, values, tile_docs):
    rows, width = queries.shape
    kv_width = keys.shape[1]
    groups = kv_width // HEAD_DIM
    heads = lax.axis_size("head")
    flops = 2 * 2 * 60 * TILE * TILE * width
    return pl.pallas_call(
        kernel,
        out_shape=jax.ShapeDtypeStruct((rows // heads, width * heads), jnp.bfloat16),
        in_specs=[pl.BlockSpec(memory_space=pltpu.SMEM)] + [pl.BlockSpec(memory_space=pl.ANY)] * 3,
        out_specs=pl.BlockSpec(memory_space=pl.ANY),
        scratch_shapes=[
            pltpu.VMEM((rows, width), jnp.bfloat16),
            pltpu.VMEM((groups, 2 * rows, HEAD_DIM), jnp.bfloat16),
            pltpu.VMEM((groups, 2 * rows, HEAD_DIM), jnp.bfloat16),
            pltpu.VMEM((2 * rows, TILE), jnp.bfloat16),
            pltpu.VMEM((16, TILE, QPK * HEAD_DIM), jnp.bfloat16),
            pltpu.SemaphoreType.DMA((2,)),
            pltpu.SemaphoreType.DMA((2, 2)),
            pltpu.SemaphoreType.DMA((2, 2)),
            pltpu.SemaphoreType.DMA((2, 2)),
            pltpu.SemaphoreType.DMA((12,)),
            pltpu.SemaphoreType.DMA((4, 2, 2)),
            pltpu.SemaphoreType.DMA((4,)),
        ],
        compiler_params=pltpu.CompilerParams(
            collective_id=0, has_side_effects=True, vmem_limit_bytes=48 << 20
        ),
        cost_estimate=pl.CostEstimate(
            flops=flops, bytes_accessed=10 << 20, transcendentals=60 * TILE * width
        ),
    )(tile_docs, queries, keys, values)


def solution(mesh):
    in_specs = (P("tok", "head"), P("tok", "head"), P("tok", "head"), P("tok"))
    out_specs = P(("tok", "head"), None)
    return jax.shard_map(local, mesh=mesh, in_specs=in_specs, out_specs=out_specs, check_vma=False)
```

```python
import functools

import jax
import jax.numpy as jnp
from jax import lax
from jax.experimental import pallas as pl
from jax.experimental.pallas import tpu as pltpu
from jax.sharding import PartitionSpec as P

HEAD_DIM = 128
QPK = 8
TILE = 128
MESH = pl.DeviceIdType.MESH
HIDDEN = -1e30
EXPONENT_SCALE = HEAD_DIM**-0.5 * 1.4426950408889634
STACK = 2
CHUNK = 256


def kernel(docs_hbm, q_hbm, k_hbm, v_hbm, out, docs, q, keys, vals, bias, stage,
           docs_sem, q_sem, kv_sem, rim_send, rim_recv, turn, send_sem, recv_sem, own_sem):
    tok, head = lax.axis_index("tok"), lax.axis_index("head")
    y_hi, core = head // 2, head % 2
    odd = tok % 2
    sibling = (tok, 2 * y_hi + 1 - core)
    across = [(tok, 2 * (1 - y_hi) + c) for c in range(2)]
    neighbour = (tok + 1 - 2 * odd, head)

    barrier = pltpu.get_barrier_semaphore()
    for device in (sibling, *across, neighbour):
        pl.semaphore_signal(barrier, inc=1, device_id=device, device_id_type=MESH)

    far, near = 4 * (1 - y_hi), 4 * y_hi

    def load_q(part):
        first = pl.multiple_of(jnp.where(part == 0, far, near) * TILE, 4 * TILE)
        rows = pl.ds(first, 4 * TILE)
        return pltpu.make_async_copy(q_hbm.at[rows], q.at[rows], q_sem.at[part])

    def load_kv(g):
        source = (slice(None), pl.ds(g * HEAD_DIM, HEAD_DIM))
        target = (g, pl.ds(7 * TILE, 8 * TILE))
        return (
            pltpu.make_async_copy(k_hbm.at[source], keys.at[target], kv_sem.at[0, g]),
            pltpu.make_async_copy(v_hbm.at[source], vals.at[target], kv_sem.at[1, g]),
        )

    def rim(g):
        source = (pl.ds(TILE, 7 * TILE), pl.ds(g * HEAD_DIM, HEAD_DIM))
        target = (g, pl.ds(0, 7 * TILE))
        return [
            pltpu.make_async_remote_copy(
                src_ref=here.at[source], dst_ref=there.at[target],
                send_sem=rim_send.at[which, g], recv_sem=rim_recv.at[which, g],
                device_id=neighbour, device_id_type=MESH,
            )
            for which, (here, there) in enumerate(((k_hbm, keys), (v_hbm, vals)))
        ]

    load_docs = pltpu.make_async_copy(docs_hbm, docs, docs_sem)
    load_docs.start()
    for copy in load_kv(0):
        copy.start()
    load_q(0).start()
    for copy in load_kv(1):
        copy.start()
    load_q(1).start()

    blank = jnp.zeros((TILE, HEAD_DIM), jnp.bfloat16)
    for g in range(2):
        keys[g, 15 * TILE :] = blank
        vals[g, 15 * TILE :] = blank

    @pl.when(odd == 0)
    def _():
        for g in range(2):
            keys[g, 6 * TILE : 7 * TILE] = blank
            vals[g, 6 * TILE : 7 * TILE] = blank

    pl.semaphore_wait(barrier, 4)

    def start_rim(g):
        for copy in rim(g):
            copy.start()

    def end_rim(g):
        for copy in rim(g):
            copy.wait_send()

    def pass_turn():
        pl.semaphore_signal(turn, inc=1, device_id=sibling, device_id_type=MESH)

    @pl.when((odd == 0) & (core == 0))
    def _():
        start_rim(0)

    def rim_step(i):
        @pl.when(core == 0)
        def _():
            @pl.when(i == 2)
            def _():
                end_rim(0)
                pass_turn()

            @pl.when(i == 4)
            def _():
                pl.semaphore_wait(turn, 1)
                start_rim(1)

            @pl.when(i == 6)
            def _():
                end_rim(1)
                pass_turn()

        @pl.when(core == 1)
        def _():
            @pl.when(i == 2)
            def _():
                pl.semaphore_wait(turn, 1)
                start_rim(0)

            @pl.when(i == 4)
            def _():
                end_rim(0)
                pass_turn()

            @pl.when(i == 6)
            def _():
                pl.semaphore_wait(turn, 1)
                start_rim(1)

            @pl.when(i == 15)
            def _():
                end_rim(1)

    eye = (
        lax.broadcasted_iota(jnp.int32, (TILE, TILE), 0)
        == lax.broadcasted_iota(jnp.int32, (TILE, TILE), 1)
    ).astype(jnp.float32).astype(jnp.bfloat16)

    def attend(i, g, t, first, chunks):
        length = chunks * CHUNK
        span = pl.ds(pl.multiple_of(first * CHUNK, CHUNK), length)
        rows = pl.ds(pl.multiple_of(t * TILE, TILE), TILE)

        for j in range(QPK // STACK):
            base = pl.multiple_of((g * QPK + j * STACK) * HEAD_DIM, STACK * HEAD_DIM)
            wide = q[rows, pl.ds(base, STACK * HEAD_DIM)]
            queries = jnp.concatenate(
                [
                    jnp.concatenate([wide[:, a * HEAD_DIM : (a + 1) * HEAD_DIM], eye], 1)
                    for a in range(STACK)
                ],
                0,
            )
            known = jnp.concatenate([keys[g, span], bias[span]], 1)
            scores = lax.dot_general(
                queries, known, (((1,), (1,)), ((), ())), preferred_element_type=jnp.float32
            )
            maxima = jnp.max(scores, axis=1, keepdims=True)
            weights = jnp.exp2((scores - maxima) * EXPONENT_SCALE).astype(jnp.bfloat16)
            summed = jnp.dot(
                weights,
                jnp.concatenate(
                    [vals[g, span], jnp.ones((length, HEAD_DIM), jnp.bfloat16)], 1
                ),
                preferred_element_type=jnp.float32,
            )
            result = (summed[:, :HEAD_DIM] / summed[:, HEAD_DIM:]).astype(jnp.bfloat16)
            stage[i, :, j * STACK * HEAD_DIM : (j + 1) * STACK * HEAD_DIM] = jnp.concatenate(
                [result[a * TILE : (a + 1) * TILE] for a in range(STACK)], 1
            )

    def place(i):
        crossing = i < 8
        g = jnp.where(crossing, i // 4, (i // 2) % 2)
        t = jnp.where(
            crossing, far + i % 4, near + 2 * jnp.where(i < 12, 1 - core, core) + i % 2
        )
        return g, t

    def send(i):
        g, t = place(i)
        return pltpu.make_async_remote_copy(
            src_ref=stage.at[i],
            dst_ref=out.at[
                pl.ds(pl.multiple_of((t % 2) * TILE, TILE), TILE),
                pl.ds(pl.multiple_of((head * 2 + g) * QPK * HEAD_DIM, QPK * HEAD_DIM), QPK * HEAD_DIM),
            ],
            send_sem=send_sem.at[i],
            recv_sem=recv_sem.at[head, g, t % 2],
            device_id=(tok, t // 2),
            device_id_type=MESH,
        )

    def keep(i):
        g, t = place(i)
        return pltpu.make_async_copy(
            stage.at[i],
            out.at[
                pl.ds(pl.multiple_of((t % 2) * TILE, TILE), TILE),
                pl.ds(pl.multiple_of((head * 2 + g) * QPK * HEAD_DIM, QPK * HEAD_DIM), QPK * HEAD_DIM),
            ],
            own_sem.at[i - 12],
        )

    def unit(i, carry):
        g, t = place(i)

        @pl.when(odd == 0)
        def _():
            rim_step(i)

        @pl.when(i % 4 == 0)
        def _():
            @pl.when(i < 8)
            def _():
                for copy in load_kv(i // 4):
                    copy.wait()

                @pl.when(odd == 1)
                def _():
                    for copy in rim(i // 4):
                        copy.wait_recv()

            @pl.when(i == 0)
            def _():
                load_docs.wait()
                load_q(0).wait()

            @pl.when(i == 8)
            def _():
                load_q(1).wait()

        reaches_back = jnp.where(t == 7, 0, odd)
        first = 3 - 3 * reaches_back
        count = (7 + t) // 2 + 1 - first
        begin = (docs[t] - 8 * tok + 7) * TILE
        row = lax.broadcasted_iota(jnp.int32, (CHUNK, TILE), 1) + (7 + t) * TILE

        def hide(c, carry):
            at = pl.multiple_of((first + c) * CHUNK, CHUNK)
            key = lax.broadcasted_iota(jnp.int32, (CHUNK, TILE), 0) + at
            bias[pl.ds(at, CHUNK)] = jnp.where(
                (key >= begin) & (key <= row), 0.0, HIDDEN
            ).astype(jnp.bfloat16)
            return carry

        lax.fori_loop(0, count, hide, 0)

        for chunks in range(1, 8):
            @pl.when(count == chunks)
            def _(chunks=chunks):
                attend(i, g, t, first, chunks)

        @pl.when(i < 12)
        def _():
            send(i).start()

        @pl.when(i >= 12)
        def _():
            keep(i).start()

        return carry

    lax.fori_loop(0, 16, unit, 0)

    def finish(i, carry):
        send(i).wait_send()
        return carry

    lax.fori_loop(0, 12, finish, 0)
    for i in range(12, 16):
        keep(i).wait()

    def arrive(n, carry):
        other = (head + 1 + n // 4) % 4
        g, half = (n // 2) % 2, n % 2
        piece = out.at[
            pl.ds(pl.multiple_of(half * TILE, TILE), TILE),
            pl.ds(pl.multiple_of((other * 2 + g) * QPK * HEAD_DIM, QPK * HEAD_DIM), QPK * HEAD_DIM),
        ]
        pltpu.make_async_remote_copy(
            src_ref=stage.at[0], dst_ref=piece, send_sem=send_sem.at[0],
            recv_sem=recv_sem.at[other, g, half], device_id=sibling, device_id_type=MESH,
        ).wait_recv()
        return carry

    lax.fori_loop(0, 12, arrive, 0)


def local(queries, keys, values, tile_docs):
    rows, width = queries.shape
    kv_width = keys.shape[1]
    groups = kv_width // HEAD_DIM
    heads = lax.axis_size("head")
    flops = 2 * 2 * 60 * TILE * TILE * width
    return pl.pallas_call(
        kernel,
        out_shape=pltpu.VMEM((rows // heads, width * heads), jnp.bfloat16),
        in_specs=[pl.BlockSpec(memory_space=pltpu.HBM)] * 4,
        out_specs=pl.BlockSpec(memory_space=pl.ANY),
        scratch_shapes=[
            pltpu.SMEM(tile_docs.shape, jnp.int32),
            pltpu.VMEM((rows, width), jnp.bfloat16),
            pltpu.VMEM((groups, 2 * rows, HEAD_DIM), jnp.bfloat16),
            pltpu.VMEM((groups, 2 * rows, HEAD_DIM), jnp.bfloat16),
            pltpu.VMEM((2 * rows, TILE), jnp.bfloat16),
            pltpu.VMEM((16, TILE, QPK * HEAD_DIM), jnp.bfloat16),
            pltpu.SemaphoreType.DMA,
            pltpu.SemaphoreType.DMA((2,)),
            pltpu.SemaphoreType.DMA((2, 2)),
            pltpu.SemaphoreType.DMA((2, 2)),
            pltpu.SemaphoreType.DMA((2, 2)),
            pltpu.SemaphoreType.REGULAR,
            pltpu.SemaphoreType.DMA((12,)),
            pltpu.SemaphoreType.DMA((4, 2, 2)),
            pltpu.SemaphoreType.DMA((4,)),
        ],
        compiler_params=pltpu.CompilerParams(
            collective_id=0, has_side_effects=True, vmem_limit_bytes=59 << 20
        ),
        cost_estimate=pl.CostEstimate(
            flops=flops, bytes_accessed=10 << 20, transcendentals=60 * TILE * width
        ),
    )(tile_docs, queries, keys, values)


def solution(mesh):
    in_specs = (P("tok", "head"), P("tok", "head"), P("tok", "head"), P("tok"))
    out_specs = P(("tok", "head"), None)
    return jax.shard_map(local, mesh=mesh, in_specs=in_specs, out_specs=out_specs, check_vma=False)
```

```python
import functools

import jax
import jax.numpy as jnp
from jax import lax
from jax.experimental import pallas as pl
from jax.experimental.pallas import tpu as pltpu
from jax.sharding import PartitionSpec as P

HEAD_DIM = 128
QPK = 8
TILE = 128
MESH = pl.DeviceIdType.MESH
HIDDEN = -1e30
EXPONENT_SCALE = HEAD_DIM**-0.5 * 1.4426950408889634
STACK = 2
CHUNK = 256
RELAYED = 1
RELAY_BLOCK = 3
PIECES = 4


def kernel(docs_hbm, q_hbm, k_hbm, v_hbm, out, docs, q, keys, vals, doc_bias, last_bias, stage,
           docs_sem, q_sem, kv_sem, rim_send, rim_recv, turn, send_sem, recv_sem, own_sem,
           lent, passed, hop_send, hop_recv):
    tok, head = lax.axis_index("tok"), lax.axis_index("head")
    y_hi, core = head // 2, head % 2
    odd = tok % 2
    sibling = (tok, 2 * y_hi + 1 - core)
    across = [(tok, 2 * (1 - y_hi) + c) for c in range(2)]
    neighbour = (tok + 1 - 2 * odd, head)

    barrier = pltpu.get_barrier_semaphore()
    for device in (sibling, *across, neighbour):
        pl.semaphore_signal(barrier, inc=1, device_id=device, device_id_type=MESH)

    far, near = 4 * (1 - y_hi), 4 * y_hi

    def load_q(part):
        first = pl.multiple_of(jnp.where(part == 0, far, near) * TILE, 4 * TILE)
        rows = pl.ds(first, 4 * TILE)
        return pltpu.make_async_copy(q_hbm.at[rows], q.at[rows], q_sem.at[part])

    def load_kv(g):
        source = (slice(None), pl.ds(g * HEAD_DIM, HEAD_DIM))
        target = (g, pl.ds(7 * TILE, 8 * TILE))
        return (
            pltpu.make_async_copy(k_hbm.at[source], keys.at[target], kv_sem.at[0, g]),
            pltpu.make_async_copy(v_hbm.at[source], vals.at[target], kv_sem.at[1, g]),
        )

    def rim(g):
        source = (pl.ds(TILE, 7 * TILE), pl.ds(g * HEAD_DIM, HEAD_DIM))
        target = (g, pl.ds(0, 7 * TILE))
        return [
            pltpu.make_async_remote_copy(
                src_ref=here.at[source], dst_ref=there.at[target],
                send_sem=rim_send.at[which, g], recv_sem=rim_recv.at[which, g],
                device_id=neighbour, device_id_type=MESH,
            )
            for which, (here, there) in enumerate(((k_hbm, keys), (v_hbm, vals)))
        ]

    load_docs = pltpu.make_async_copy(docs_hbm, docs, docs_sem)
    load_docs.start()
    for copy in load_kv(0):
        copy.start()
    load_q(0).start()
    for copy in load_kv(1):
        copy.start()
    load_q(1).start()

    blank = jnp.zeros((TILE, HEAD_DIM), jnp.bfloat16)
    for g in range(2):
        keys[g, 15 * TILE :] = blank
        vals[g, 15 * TILE :] = blank

    @pl.when(odd == 0)
    def _():
        for g in range(2):
            keys[g, 6 * TILE : 7 * TILE] = blank
            vals[g, 6 * TILE : 7 * TILE] = blank

    pl.semaphore_wait(barrier, 4)

    def start_rim(g):
        for copy in rim(g):
            copy.start()

    def end_rim(g):
        for copy in rim(g):
            copy.wait_send()

    def pass_turn():
        pl.semaphore_signal(turn, inc=1, device_id=sibling, device_id_type=MESH)

    @pl.when((odd == 0) & (core == 0))
    def _():
        start_rim(0)

    def rim_step(b):
        @pl.when(core == 0)
        def _():
            @pl.when(b == 1)
            def _():
                end_rim(0)
                pass_turn()

            @pl.when(b == 2)
            def _():
                pl.semaphore_wait(turn, 1)
                start_rim(1)

            @pl.when(b == 3)
            def _():
                end_rim(1)
                pass_turn()

        @pl.when(core == 1)
        def _():
            @pl.when(b == 1)
            def _():
                pl.semaphore_wait(turn, 1)
                start_rim(0)

            @pl.when(b == 2)
            def _():
                end_rim(0)
                pass_turn()

            @pl.when(b == 3)
            def _():
                pl.semaphore_wait(turn, 1)
                start_rim(1)

            @pl.when(b == 7)
            def _():
                end_rim(1)

    def attend(i, g, parts):
        items = [(u, j) for u in range(len(parts)) for j in range(QPK // STACK)]

        def reach(u):
            _, first, chunks = parts[u]
            return pl.multiple_of(first * CHUNK, CHUNK), chunks * CHUNK

        def score(u, j):
            at, length = reach(u)
            rows = pl.ds(pl.multiple_of(parts[u][0] * TILE, TILE), TILE)
            base = pl.multiple_of((g * QPK + j * STACK) * HEAD_DIM, STACK * HEAD_DIM)
            wide = q[rows, pl.ds(base, STACK * HEAD_DIM)]
            scores = lax.dot_general(
                jnp.concatenate(
                    [wide[:, a * HEAD_DIM : (a + 1) * HEAD_DIM] for a in range(STACK)], 0
                ),
                keys[g, pl.ds(at, length)],
                (((1,), (1,)), ((), ())),
                preferred_element_type=jnp.float32,
            )
            body = length - CHUNK
            tail = scores[:, body:] + jnp.concatenate([last_bias[u]] * STACK, 0)
            if body == 0:
                return tail
            return jnp.concatenate(
                [scores[:, :body] + doc_bias[u : u + 1, pl.ds(at, body)], tail], 1
            )

        def finish(u, j, scores):
            at, length = reach(u)
            maxima = jnp.max(scores, axis=1, keepdims=True)
            weights = jnp.exp2((scores - maxima) * EXPONENT_SCALE).astype(jnp.bfloat16)
            summed = jnp.dot(
                weights,
                jnp.concatenate(
                    [vals[g, pl.ds(at, length)], jnp.ones((length, HEAD_DIM), jnp.bfloat16)], 1
                ),
                preferred_element_type=jnp.float32,
            )
            result = (summed[:, :HEAD_DIM] / summed[:, HEAD_DIM:]).astype(jnp.bfloat16)
            stage[i + u, :, j * STACK * HEAD_DIM : (j + 1) * STACK * HEAD_DIM] = jnp.concatenate(
                [result[a * TILE : (a + 1) * TILE] for a in range(STACK)], 1
            )

        scores = score(*items[0])
        for n, item in enumerate(items):
            ahead = score(*items[n + 1]) if n + 1 < len(items) else None
            finish(*item, scores)
            scores = ahead
            if item == (0, QPK // STACK - 1):
                dispatch(i)

    def place(i):
        crossing = i < 8
        g = jnp.where(crossing, i // 4, (i // 2) % 2)
        t = jnp.where(
            crossing, far + (i + 2 * core) % 4, near + 2 * jnp.where(i < 12, 1 - core, core) + i % 2
        )
        return g, t

    def send(i):
        g, t = place(i)
        return pltpu.make_async_remote_copy(
            src_ref=stage.at[i],
            dst_ref=out.at[
                pl.ds(pl.multiple_of((t % 2) * TILE, TILE), TILE),
                pl.ds(pl.multiple_of((head * 2 + g) * QPK * HEAD_DIM, QPK * HEAD_DIM), QPK * HEAD_DIM),
            ],
            send_sem=send_sem.at[i],
            recv_sem=recv_sem.at[head, g, t % 2],
            device_id=(tok, t // 2),
            device_id_type=MESH,
        )

    def keep(i):
        g, t = place(i)
        return pltpu.make_async_copy(
            stage.at[i],
            out.at[
                pl.ds(pl.multiple_of((t % 2) * TILE, TILE), TILE),
                pl.ds(pl.multiple_of((head * 2 + g) * QPK * HEAD_DIM, QPK * HEAD_DIM), QPK * HEAD_DIM),
            ],
            own_sem.at[i - 12],
        )

    def hop(n, p):
        rows = pl.ds(p * (TILE // PIECES), TILE // PIECES)
        opposite = (tok, (head + 2) % 4)
        column = pl.multiple_of((head + 2) % 4 * 2 * QPK * HEAD_DIM, QPK * HEAD_DIM)
        source, target, device = (
            (stage.at[RELAYED, rows], lent.at[rows], neighbour),
            (lent.at[rows], passed.at[rows], opposite),
            (
                passed.at[rows],
                out.at[
                    pl.ds(TILE + p * (TILE // PIECES), TILE // PIECES),
                    pl.ds(column, QPK * HEAD_DIM),
                ],
                neighbour,
            ),
        )[n]
        return pltpu.make_async_remote_copy(
            src_ref=source, dst_ref=target, send_sem=hop_send.at[n, p], recv_sem=hop_recv.at[n, p],
            device_id=device, device_id_type=MESH,
        )

    def dispatch(i):
        relayed = (odd == 1) & (i == RELAYED)

        @pl.when((i < 12) & jnp.logical_not(relayed))
        def _():
            send(i).start()

        @pl.when(relayed)
        def _():
            for p in range(PIECES):
                hop(0, p).start()

        @pl.when(i >= 12)
        def _():
            keep(i).start()

    def block(b, carry):
        i = 2 * b
        g = place(i)[0]

        @pl.when(odd == 0)
        def _():
            rim_step(b)

        @pl.when((b == RELAY_BLOCK) & (odd == 0))
        def _():
            for p in range(PIECES):
                hop(0, p).wait_recv()
                hop(1, p).start()

        @pl.when((b == 0) | (b == 2))
        def _():
            for copy in load_kv(b // 2):
                copy.wait()

            @pl.when(odd == 1)
            def _():
                for copy in rim(b // 2):
                    copy.wait_recv()

        @pl.when(b == 0)
        def _():
            load_docs.wait()
            load_q(0).wait()

        @pl.when(b == 4)
        def _():
            load_q(1).wait()

        parts = []
        for u in range(2):
            t = place(i + u)[1]
            reaches_back = jnp.where(t == 7, 0, odd)
            first = 3 - 3 * reaches_back
            count = (7 + t) // 2 + 1 - first
            begin = (docs[t] - 8 * tok + 7) * TILE
            doc_bias[u : u + 1, :] = jnp.where(
                lax.broadcasted_iota(jnp.int32, (1, doc_bias.shape[1]), 1) >= begin, 0.0, HIDDEN
            )
            key = lax.broadcasted_iota(jnp.int32, (TILE, CHUNK), 1) + (first + count - 1) * CHUNK
            row = lax.broadcasted_iota(jnp.int32, (TILE, CHUNK), 0) + (7 + t) * TILE
            last_bias[u] = jnp.where((key >= begin) & (key <= row), 0.0, HIDDEN)
            parts.append((t, first, count))

        for counts in ((1, 2), (2, 3), (3, 4), (4, 5), (5, 6), (6, 7), (7, 5)):
            @pl.when(parts[0][2] == counts[0])
            def _(counts=counts):
                attend(i, g, [(t, first, n) for (t, first, _), n in zip(parts, counts)])

        dispatch(i + 1)

        return carry

    lax.fori_loop(0, 8, block, 0)

    @pl.when(odd == 0)
    def _():
        for p in range(PIECES):
            hop(1, p).wait_recv()
            hop(2, p).start()

    def finish(i, carry):
        @pl.when((odd == 0) | (i != RELAYED))
        def _():
            send(i).wait_send()

        return carry

    lax.fori_loop(0, 12, finish, 0)
    for i in range(12, 16):
        keep(i).wait()

    def arrive(n, carry):
        other = (head + 1 + n // 4) % 4
        g, half = (n // 2) % 2, n % 2
        piece = out.at[
            pl.ds(pl.multiple_of(half * TILE, TILE), TILE),
            pl.ds(pl.multiple_of((other * 2 + g) * QPK * HEAD_DIM, QPK * HEAD_DIM), QPK * HEAD_DIM),
        ]

        @pl.when((odd == 0) | (n != 5))
        def _():
            pltpu.make_async_remote_copy(
                src_ref=stage.at[0], dst_ref=piece, send_sem=send_sem.at[0],
                recv_sem=recv_sem.at[other, g, half], device_id=sibling, device_id_type=MESH,
            ).wait_recv()

        return carry

    lax.fori_loop(0, 12, arrive, 0)

    @pl.when(odd == 0)
    def _():
        for p in range(PIECES):
            hop(1, p).wait_send()
            hop(2, p).wait_send()

    @pl.when(odd == 1)
    def _():
        for p in range(PIECES):
            hop(0, p).wait_send()
            hop(2, p).wait_recv()


def local(queries, keys, values, tile_docs):
    rows, width = queries.shape
    kv_width = keys.shape[1]
    groups = kv_width // HEAD_DIM
    heads = lax.axis_size("head")
    flops = 2 * 2 * 60 * TILE * TILE * width
    return pl.pallas_call(
        kernel,
        out_shape=pltpu.VMEM((rows // heads, width * heads), jnp.bfloat16),
        in_specs=[pl.BlockSpec(memory_space=pltpu.HBM)] * 4,
        out_specs=pl.BlockSpec(memory_space=pl.ANY),
        scratch_shapes=[
            pltpu.SMEM(tile_docs.shape, jnp.int32),
            pltpu.VMEM((rows, width), jnp.bfloat16),
            pltpu.VMEM((groups, 2 * rows, HEAD_DIM), jnp.bfloat16),
            pltpu.VMEM((groups, 2 * rows, HEAD_DIM), jnp.bfloat16),
            pltpu.VMEM((8, 2 * rows), jnp.float32),
            pltpu.VMEM((2, TILE, CHUNK), jnp.float32),
            pltpu.VMEM((16, TILE, QPK * HEAD_DIM), jnp.bfloat16),
            pltpu.SemaphoreType.DMA,
            pltpu.SemaphoreType.DMA((2,)),
            pltpu.SemaphoreType.DMA((2, 2)),
            pltpu.SemaphoreType.DMA((2, 2)),
            pltpu.SemaphoreType.DMA((2, 2)),
            pltpu.SemaphoreType.REGULAR,
            pltpu.SemaphoreType.DMA((12,)),
            pltpu.SemaphoreType.DMA((4, 2, 2)),
            pltpu.SemaphoreType.DMA((4,)),
            pltpu.VMEM((TILE, QPK * HEAD_DIM), jnp.bfloat16),
            pltpu.VMEM((TILE, QPK * HEAD_DIM), jnp.bfloat16),
            pltpu.SemaphoreType.DMA((3, PIECES)),
            pltpu.SemaphoreType.DMA((3, PIECES)),
        ],
        compiler_params=pltpu.CompilerParams(
            collective_id=0, has_side_effects=True, vmem_limit_bytes=59 << 20
        ),
        cost_estimate=pl.CostEstimate(
            flops=flops, bytes_accessed=10 << 20, transcendentals=60 * TILE * width
        ),
    )(tile_docs, queries, keys, values)


def solution(mesh):
    in_specs = (P("tok", "head"), P("tok", "head"), P("tok", "head"), P("tok"))
    out_specs = P(("tok", "head"), None)
    return jax.shard_map(local, mesh=mesh, in_specs=in_specs, out_specs=out_specs, check_vma=False)
```

```python
import functools

import jax
import jax.numpy as jnp
from jax import lax
from jax.experimental import pallas as pl
from jax.experimental.pallas import tpu as pltpu
from jax.sharding import PartitionSpec as P

HEAD_DIM = 128
QPK = 8
TILE = 128
MESH = pl.DeviceIdType.MESH
HIDDEN = -1e30
EXPONENT_SCALE = HEAD_DIM**-0.5 * 1.4426950408889634
STACK = 2
CHUNK = 256
RELAY_BLOCK = 3
PIECES = 3
KEPT = 32
PIECE = (TILE - KEPT) // PIECES


def kernel(docs_hbm, q_hbm, k_hbm, v_hbm, out, docs, q, keys, vals, doc_bias, last_bias, stage,
           docs_sem, q_sem, kv_sem, rim_send, rim_recv, turn, send_sem, recv_sem, own_sem,
           lent, passed, hop_send, hop_recv):
    tok, head = lax.axis_index("tok"), lax.axis_index("head")
    y_hi, core = head // 2, head % 2
    odd = tok % 2
    sibling = (tok, 2 * y_hi + 1 - core)
    across = [(tok, 2 * (1 - y_hi) + c) for c in range(2)]
    neighbour = (tok + 1 - 2 * odd, head)

    barrier = pltpu.get_barrier_semaphore()
    for device in (sibling, *across, neighbour):
        pl.semaphore_signal(barrier, inc=1, device_id=device, device_id_type=MESH)

    far, near = 4 * (1 - y_hi), 4 * y_hi

    def load_q(part):
        first, tiles = (
            (far + 2 * odd, 2), (far + 2 - 2 * odd, 2), (near, 4)
        )[part]
        rows = pl.ds(pl.multiple_of(first * TILE, 2 * TILE), tiles * TILE)
        return pltpu.make_async_copy(q_hbm.at[rows], q.at[rows], q_sem.at[part])

    def load_kv(g):
        source = (slice(None), pl.ds(g * HEAD_DIM, HEAD_DIM))
        target = (g, pl.ds(7 * TILE, 8 * TILE))
        return (
            pltpu.make_async_copy(k_hbm.at[source], keys.at[target], kv_sem.at[0, g]),
            pltpu.make_async_copy(v_hbm.at[source], vals.at[target], kv_sem.at[1, g]),
        )

    def rim(g):
        source = (pl.ds(TILE, 7 * TILE), pl.ds(g * HEAD_DIM, HEAD_DIM))
        target = (g, pl.ds(0, 7 * TILE))
        return [
            pltpu.make_async_remote_copy(
                src_ref=here.at[source], dst_ref=there.at[target],
                send_sem=rim_send.at[which, g], recv_sem=rim_recv.at[which, g],
                device_id=neighbour, device_id_type=MESH,
            )
            for which, (here, there) in enumerate(((k_hbm, keys), (v_hbm, vals)))
        ]

    load_docs = pltpu.make_async_copy(docs_hbm, docs, docs_sem)
    load_docs.start()
    for copy in load_kv(0):
        copy.start()
    load_q(0).start()
    load_q(1).start()
    for copy in load_kv(1):
        copy.start()
    load_q(2).start()

    blank = jnp.zeros((TILE, HEAD_DIM), jnp.bfloat16)
    for g in range(2):
        keys[g, 15 * TILE :] = blank
        vals[g, 15 * TILE :] = blank

    @pl.when(odd == 0)
    def _():
        for g in range(2):
            keys[g, 6 * TILE : 7 * TILE] = blank
            vals[g, 6 * TILE : 7 * TILE] = blank

    pl.semaphore_wait(barrier, 4)

    def start_rim(g):
        for copy in rim(g):
            copy.start()

    def end_rim(g):
        for copy in rim(g):
            copy.wait_send()

    def pass_turn():
        pl.semaphore_signal(turn, inc=1, device_id=sibling, device_id_type=MESH)

    @pl.when((odd == 0) & (core == 0))
    def _():
        start_rim(0)

    def rim_step(b):
        @pl.when(core == 0)
        def _():
            @pl.when(b == 1)
            def _():
                end_rim(0)
                pass_turn()

            @pl.when(b == 2)
            def _():
                pl.semaphore_wait(turn, 1)
                start_rim(1)

            @pl.when(b == 3)
            def _():
                end_rim(1)
                pass_turn()

        @pl.when(core == 1)
        def _():
            @pl.when(b == 1)
            def _():
                pl.semaphore_wait(turn, 1)
                start_rim(0)

            @pl.when(b == 2)
            def _():
                end_rim(0)
                pass_turn()

            @pl.when(b == 3)
            def _():
                pl.semaphore_wait(turn, 1)
                start_rim(1)

            @pl.when(b == 7)
            def _():
                end_rim(1)

    def attend(i, g, parts):
        items = [(u, j) for u in range(len(parts)) for j in range(QPK // STACK)]

        def reach(u):
            _, first, chunks = parts[u]
            return pl.multiple_of(first * CHUNK, CHUNK), chunks * CHUNK

        def score(u, j):
            at, length = reach(u)
            rows = pl.ds(pl.multiple_of(parts[u][0] * TILE, TILE), TILE)
            base = pl.multiple_of((g * QPK + j * STACK) * HEAD_DIM, STACK * HEAD_DIM)
            wide = q[rows, pl.ds(base, STACK * HEAD_DIM)]
            scores = lax.dot_general(
                jnp.concatenate(
                    [wide[:, a * HEAD_DIM : (a + 1) * HEAD_DIM] for a in range(STACK)], 0
                ),
                keys[g, pl.ds(at, length)],
                (((1,), (1,)), ((), ())),
                preferred_element_type=jnp.float32,
            )
            body = length - CHUNK
            tail = scores[:, body:] + jnp.concatenate([last_bias[u]] * STACK, 0)
            if body == 0:
                return tail
            return jnp.concatenate(
                [scores[:, :body] + doc_bias[u : u + 1, pl.ds(at, body)], tail], 1
            )

        def finish(u, j, scores):
            at, length = reach(u)
            maxima = jnp.max(scores, axis=1, keepdims=True)
            weights = jnp.exp2((scores - maxima) * EXPONENT_SCALE).astype(jnp.bfloat16)
            summed = jnp.dot(
                weights,
                jnp.concatenate(
                    [vals[g, pl.ds(at, length)], jnp.ones((length, HEAD_DIM), jnp.bfloat16)], 1
                ),
                preferred_element_type=jnp.float32,
            )
            result = (summed[:, :HEAD_DIM] / summed[:, HEAD_DIM:]).astype(jnp.bfloat16)
            stage[i + u, :, j * STACK * HEAD_DIM : (j + 1) * STACK * HEAD_DIM] = jnp.concatenate(
                [result[a * TILE : (a + 1) * TILE] for a in range(STACK)], 1
            )

        scores = score(*items[0])
        for n, item in enumerate(items):
            ahead = score(*items[n + 1]) if n + 1 < len(items) else None
            finish(*item, scores)
            scores = ahead
            if item == (0, QPK // STACK - 1):
                dispatch(i)

    def place(i):
        crossing = i < 8
        g = jnp.where(crossing, i // 4, (i // 2) % 2)
        t = jnp.where(
            crossing, far + (i + 2 * odd) % 4, near + 2 * jnp.where(i < 12, 1 - core, core) + i % 2
        )
        return g, t

    def send(i, rows=TILE):
        g, t = place(i)
        return pltpu.make_async_remote_copy(
            src_ref=stage.at[i, pl.ds(0, rows)],
            dst_ref=out.at[
                pl.ds(pl.multiple_of((t % 2) * TILE, TILE), rows),
                pl.ds(pl.multiple_of((head * 2 + g) * QPK * HEAD_DIM, QPK * HEAD_DIM), QPK * HEAD_DIM),
            ],
            send_sem=send_sem.at[i],
            recv_sem=recv_sem.at[head, g, t % 2],
            device_id=(tok, t // 2),
            device_id_type=MESH,
        )

    def keep(i):
        g, t = place(i)
        return pltpu.make_async_copy(
            stage.at[i],
            out.at[
                pl.ds(pl.multiple_of((t % 2) * TILE, TILE), TILE),
                pl.ds(pl.multiple_of((head * 2 + g) * QPK * HEAD_DIM, QPK * HEAD_DIM), QPK * HEAD_DIM),
            ],
            own_sem.at[i - 12],
        )

    relay_unit = 3 - 2 * core

    def hop(n, p):
        rows = pl.ds(KEPT + p * PIECE, PIECE)
        opposite = (tok, (head + 2) % 4)
        column = pl.multiple_of((head + 2) % 4 * 2 * QPK * HEAD_DIM, QPK * HEAD_DIM)
        source, target, device = (
            (stage.at[relay_unit, rows], lent.at[rows], neighbour),
            (lent.at[rows], passed.at[rows], opposite),
            (
                passed.at[rows],
                out.at[
                    pl.ds(TILE + KEPT + p * PIECE, PIECE),
                    pl.ds(column, QPK * HEAD_DIM),
                ],
                neighbour,
            ),
        )[n]
        return pltpu.make_async_remote_copy(
            src_ref=source, dst_ref=target, send_sem=hop_send.at[n, p], recv_sem=hop_recv.at[n, p],
            device_id=device, device_id_type=MESH,
        )

    def dispatch(i):
        relayed = (odd == 1) & (i == relay_unit)

        @pl.when((i < 12) & jnp.logical_not(relayed))
        def _():
            send(i).start()

        @pl.when(relayed)
        def _():
            send(i, KEPT).start()
            for p in range(PIECES):
                hop(0, p).start()

        @pl.when(i >= 12)
        def _():
            keep(i).start()

    def block(b, carry):
        i = 2 * b
        g = place(i)[0]

        @pl.when(odd == 0)
        def _():
            rim_step(b)

        @pl.when((b == RELAY_BLOCK) & (odd == 0))
        def _():
            for p in range(PIECES):
                hop(0, p).wait_recv()
                hop(1, p).start()

        @pl.when((b == 0) | (b == 2))
        def _():
            for copy in load_kv(b // 2):
                copy.wait()

            @pl.when(odd == 1)
            def _():
                for copy in rim(b // 2):
                    copy.wait_recv()

        @pl.when(b == 0)
        def _():
            load_docs.wait()
            load_q(0).wait()

        @pl.when(b == 1)
        def _():
            load_q(1).wait()

        @pl.when(b == 4)
        def _():
            load_q(2).wait()

        parts = []
        for u in range(2):
            t = place(i + u)[1]
            reaches_back = jnp.where(t == 7, 0, odd)
            first = 3 - 3 * reaches_back
            count = (7 + t) // 2 + 1 - first
            begin = (docs[t] - 8 * tok + 7) * TILE
            doc_bias[u : u + 1, :] = jnp.where(
                lax.broadcasted_iota(jnp.int32, (1, doc_bias.shape[1]), 1) >= begin, 0.0, HIDDEN
            )
            key = lax.broadcasted_iota(jnp.int32, (TILE, CHUNK), 1) + (first + count - 1) * CHUNK
            row = lax.broadcasted_iota(jnp.int32, (TILE, CHUNK), 0) + (7 + t) * TILE
            last_bias[u] = jnp.where((key >= begin) & (key <= row), 0.0, HIDDEN)
            parts.append((t, first, count))

        for counts in ((1, 2), (2, 3), (3, 4), (4, 5), (5, 6), (6, 7), (7, 5)):
            @pl.when(parts[0][2] == counts[0])
            def _(counts=counts):
                attend(i, g, [(t, first, n) for (t, first, _), n in zip(parts, counts)])

        dispatch(i + 1)

        return carry

    lax.fori_loop(0, 8, block, 0)

    @pl.when(odd == 0)
    def _():
        for p in range(PIECES):
            hop(1, p).wait_recv()
            hop(2, p).start()

    def finish(i, carry):
        relayed = (odd == 1) & (i == relay_unit)

        @pl.when(jnp.logical_not(relayed))
        def _():
            send(i).wait_send()

        @pl.when(relayed)
        def _():
            send(i, KEPT).wait_send()

        return carry

    lax.fori_loop(0, 12, finish, 0)
    for i in range(12, 16):
        keep(i).wait()

    def arrive(n, carry):
        other = (head + 1 + n // 4) % 4
        g, half = (n // 2) % 2, n % 2

        def arrival(rows):
            return pltpu.make_async_remote_copy(
                src_ref=stage.at[0, pl.ds(0, rows)],
                dst_ref=out.at[
                    pl.ds(pl.multiple_of(half * TILE, TILE), rows),
                    pl.ds(pl.multiple_of((other * 2 + g) * QPK * HEAD_DIM, QPK * HEAD_DIM), QPK * HEAD_DIM),
                ],
                send_sem=send_sem.at[0],
                recv_sem=recv_sem.at[other, g, half],
                device_id=sibling,
                device_id_type=MESH,
            )

        relayed = (odd == 1) & (n == 5)

        @pl.when(jnp.logical_not(relayed))
        def _():
            arrival(TILE).wait_recv()

        @pl.when(relayed)
        def _():
            arrival(KEPT).wait_recv()

        return carry

    lax.fori_loop(0, 12, arrive, 0)

    @pl.when(odd == 0)
    def _():
        for p in range(PIECES):
            hop(1, p).wait_send()
            hop(2, p).wait_send()

    @pl.when(odd == 1)
    def _():
        for p in range(PIECES):
            hop(0, p).wait_send()
            hop(2, p).wait_recv()


def local(queries, keys, values, tile_docs):
    rows, width = queries.shape
    kv_width = keys.shape[1]
    groups = kv_width // HEAD_DIM
    heads = lax.axis_size("head")
    flops = 2 * 2 * 60 * TILE * TILE * width
    return pl.pallas_call(
        kernel,
        out_shape=pltpu.VMEM((rows // heads, width * heads), jnp.bfloat16),
        in_specs=[pl.BlockSpec(memory_space=pltpu.HBM)] * 4,
        out_specs=pl.BlockSpec(memory_space=pl.ANY),
        scratch_shapes=[
            pltpu.SMEM(tile_docs.shape, jnp.int32),
            pltpu.VMEM((rows, width), jnp.bfloat16),
            pltpu.VMEM((groups, 2 * rows, HEAD_DIM), jnp.bfloat16),
            pltpu.VMEM((groups, 2 * rows, HEAD_DIM), jnp.bfloat16),
            pltpu.VMEM((8, 2 * rows), jnp.float32),
            pltpu.VMEM((2, TILE, CHUNK), jnp.float32),
            pltpu.VMEM((16, TILE, QPK * HEAD_DIM), jnp.bfloat16),
            pltpu.SemaphoreType.DMA,
            pltpu.SemaphoreType.DMA((3,)),
            pltpu.SemaphoreType.DMA((2, 2)),
            pltpu.SemaphoreType.DMA((2, 2)),
            pltpu.SemaphoreType.DMA((2, 2)),
            pltpu.SemaphoreType.REGULAR,
            pltpu.SemaphoreType.DMA((12,)),
            pltpu.SemaphoreType.DMA((4, 2, 2)),
            pltpu.SemaphoreType.DMA((4,)),
            pltpu.VMEM((TILE, QPK * HEAD_DIM), jnp.bfloat16),
            pltpu.VMEM((TILE, QPK * HEAD_DIM), jnp.bfloat16),
            pltpu.SemaphoreType.DMA((3, PIECES)),
            pltpu.SemaphoreType.DMA((3, PIECES)),
        ],
        compiler_params=pltpu.CompilerParams(
            collective_id=0, has_side_effects=True, vmem_limit_bytes=59 << 20
        ),
        cost_estimate=pl.CostEstimate(
            flops=flops, bytes_accessed=10 << 20, transcendentals=60 * TILE * width
        ),
    )(tile_docs, queries, keys, values)


def solution(mesh):
    in_specs = (P("tok", "head"), P("tok", "head"), P("tok", "head"), P("tok"))
    out_specs = P(("tok", "head"), None)
    return jax.shard_map(local, mesh=mesh, in_specs=in_specs, out_specs=out_specs, check_vma=False)
```

```python
import functools

import jax
import jax.numpy as jnp
from jax import lax
from jax.experimental import pallas as pl
from jax.experimental.pallas import tpu as pltpu
from jax.sharding import PartitionSpec as P

HEAD_DIM = 128
QPK = 8
TILE = 128
MESH = pl.DeviceIdType.MESH
HIDDEN = -1e30
EXPONENT_SCALE = HEAD_DIM**-0.5 * 1.4426950408889634
STACK = 2
CHUNK = 256
RELAY_BLOCK = 3
PIECES = 3
KEPT = 32
PIECE = (TILE - KEPT) // PIECES


def kernel(docs_hbm, q_hbm, k_hbm, v_hbm, out, docs, q, keys, vals, doc_bias, last_bias, stage,
           docs_sem, q_sem, kv_sem, rim_send, rim_recv, turn, send_sem, recv_sem, own_sem,
           lent, passed, hop_send, hop_recv):
    tok, head = lax.axis_index("tok"), lax.axis_index("head")
    y_hi, core = head // 2, head % 2
    odd = tok % 2
    sibling = (tok, 2 * y_hi + 1 - core)
    across = [(tok, 2 * (1 - y_hi) + c) for c in range(2)]
    neighbour = (tok + 1 - 2 * odd, head)

    barrier = pltpu.get_barrier_semaphore()
    for device in (sibling, *across, neighbour):
        pl.semaphore_signal(barrier, inc=1, device_id=device, device_id_type=MESH)

    far, near = 4 * (1 - y_hi), 4 * y_hi

    def load_q(part):
        first, tiles = (
            (far + 2 * odd, 2), (far + 2 - 2 * odd, 2), (near, 4)
        )[part]
        rows = pl.ds(pl.multiple_of(first * TILE, 2 * TILE), tiles * TILE)
        return pltpu.make_async_copy(q_hbm.at[rows], q.at[rows], q_sem.at[part])

    def load_kv(g):
        source = (slice(None), pl.ds(g * HEAD_DIM, HEAD_DIM))
        target = (g, pl.ds(7 * TILE, 8 * TILE))
        return (
            pltpu.make_async_copy(k_hbm.at[source], keys.at[target], kv_sem.at[0, g]),
            pltpu.make_async_copy(v_hbm.at[source], vals.at[target], kv_sem.at[1, g]),
        )

    def rim(g):
        source = (pl.ds(TILE, 7 * TILE), pl.ds(g * HEAD_DIM, HEAD_DIM))
        target = (g, pl.ds(0, 7 * TILE))
        return [
            pltpu.make_async_remote_copy(
                src_ref=here.at[source], dst_ref=there.at[target],
                send_sem=rim_send.at[which, g], recv_sem=rim_recv.at[which, g],
                device_id=neighbour, device_id_type=MESH,
            )
            for which, (here, there) in enumerate(((k_hbm, keys), (v_hbm, vals)))
        ]

    load_docs = pltpu.make_async_copy(docs_hbm, docs, docs_sem)
    load_docs.start()
    for copy in load_kv(0):
        copy.start()
    load_q(0).start()
    load_q(1).start()
    for copy in load_kv(1):
        copy.start()
    load_q(2).start()

    blank = jnp.zeros((TILE, HEAD_DIM), jnp.bfloat16)
    for g in range(2):
        keys[g, 15 * TILE :] = blank
        vals[g, 15 * TILE :] = blank

    @pl.when(odd == 0)
    def _():
        for g in range(2):
            keys[g, 6 * TILE : 7 * TILE] = blank
            vals[g, 6 * TILE : 7 * TILE] = blank

    pl.semaphore_wait(barrier, 4)

    def start_rim(g):
        for copy in rim(g):
            copy.start()

    def end_rim(g):
        for copy in rim(g):
            copy.wait_send()

    def pass_turn():
        pl.semaphore_signal(turn, inc=1, device_id=sibling, device_id_type=MESH)

    @pl.when((odd == 0) & (core == 0))
    def _():
        start_rim(0)

    def rim_step(b):
        @pl.when(core == 0)
        def _():
            @pl.when(b == 1)
            def _():
                end_rim(0)
                pass_turn()

            @pl.when(b == 2)
            def _():
                pl.semaphore_wait(turn, 1)
                start_rim(1)

            @pl.when(b == 3)
            def _():
                end_rim(1)
                pass_turn()

        @pl.when(core == 1)
        def _():
            @pl.when(b == 1)
            def _():
                pl.semaphore_wait(turn, 1)
                start_rim(0)

            @pl.when(b == 2)
            def _():
                end_rim(0)
                pass_turn()

            @pl.when(b == 3)
            def _():
                pl.semaphore_wait(turn, 1)
                start_rim(1)

            @pl.when(b == 7)
            def _():
                end_rim(1)

    def ready(g, which):
        load_kv(g)[which].wait()

        @pl.when(odd == 1)
        def _():
            rim(g)[which].wait_recv()

    def attend(i, g, parts):
        items = [(u, j) for u in range(len(parts)) for j in range(QPK // STACK)]

        def reach(u):
            _, first, chunks = parts[u]
            return pl.multiple_of(first * CHUNK, CHUNK), chunks * CHUNK

        def score(u, j):
            at, length = reach(u)
            rows = pl.ds(pl.multiple_of(parts[u][0] * TILE, TILE), TILE)
            base = pl.multiple_of((g * QPK + j * STACK) * HEAD_DIM, STACK * HEAD_DIM)
            wide = q[rows, pl.ds(base, STACK * HEAD_DIM)]
            scores = lax.dot_general(
                jnp.concatenate(
                    [wide[:, a * HEAD_DIM : (a + 1) * HEAD_DIM] for a in range(STACK)], 0
                ),
                keys[g, pl.ds(at, length)],
                (((1,), (1,)), ((), ())),
                preferred_element_type=jnp.float32,
            )
            body = length - CHUNK
            tail = scores[:, body:] + jnp.concatenate([last_bias[u]] * STACK, 0)
            if body == 0:
                return tail
            return jnp.concatenate(
                [scores[:, :body] + doc_bias[u : u + 1, pl.ds(at, body)], tail], 1
            )

        def finish(u, j, scores):
            at, length = reach(u)
            maxima = jnp.max(scores, axis=1, keepdims=True)
            weights = jnp.exp2((scores - maxima) * EXPONENT_SCALE).astype(jnp.bfloat16)
            summed = jnp.dot(
                weights,
                jnp.concatenate(
                    [vals[g, pl.ds(at, length)], jnp.ones((length, HEAD_DIM), jnp.bfloat16)], 1
                ),
                preferred_element_type=jnp.float32,
            )
            result = (summed[:, :HEAD_DIM] / summed[:, HEAD_DIM:]).astype(jnp.bfloat16)
            stage[i + u, :, j * STACK * HEAD_DIM : (j + 1) * STACK * HEAD_DIM] = jnp.concatenate(
                [result[a * TILE : (a + 1) * TILE] for a in range(STACK)], 1
            )

        scores = score(*items[0])
        for n, item in enumerate(items):
            ahead = score(*items[n + 1]) if n + 1 < len(items) else None
            if n == 0:
                @pl.when((i == 0) | (i == 4))
                def _():
                    ready(i // 4, 1)
            finish(*item, scores)
            scores = ahead
            if item == (0, QPK // STACK - 1):
                dispatch(i)

    def place(i):
        crossing = i < 8
        g = jnp.where(crossing, i // 4, (i // 2) % 2)
        t = jnp.where(
            crossing, far + (i + 2 * odd) % 4, near + 2 * jnp.where(i < 12, 1 - core, core) + i % 2
        )
        return g, t

    def send(i, rows=TILE):
        g, t = place(i)
        return pltpu.make_async_remote_copy(
            src_ref=stage.at[i, pl.ds(0, rows)],
            dst_ref=out.at[
                pl.ds(pl.multiple_of((t % 2) * TILE, TILE), rows),
                pl.ds(pl.multiple_of((head * 2 + g) * QPK * HEAD_DIM, QPK * HEAD_DIM), QPK * HEAD_DIM),
            ],
            send_sem=send_sem.at[i],
            recv_sem=recv_sem.at[head, g, t % 2],
            device_id=(tok, t // 2),
            device_id_type=MESH,
        )

    def keep(i):
        g, t = place(i)
        return pltpu.make_async_copy(
            stage.at[i],
            out.at[
                pl.ds(pl.multiple_of((t % 2) * TILE, TILE), TILE),
                pl.ds(pl.multiple_of((head * 2 + g) * QPK * HEAD_DIM, QPK * HEAD_DIM), QPK * HEAD_DIM),
            ],
            own_sem.at[i - 12],
        )

    relay_unit = 3 - 2 * core

    def hop(n, p):
        rows = pl.ds(KEPT + p * PIECE, PIECE)
        opposite = (tok, (head + 2) % 4)
        column = pl.multiple_of((head + 2) % 4 * 2 * QPK * HEAD_DIM, QPK * HEAD_DIM)
        source, target, device = (
            (stage.at[relay_unit, rows], lent.at[rows], neighbour),
            (lent.at[rows], passed.at[rows], opposite),
            (
                passed.at[rows],
                out.at[
                    pl.ds(TILE + KEPT + p * PIECE, PIECE),
                    pl.ds(column, QPK * HEAD_DIM),
                ],
                neighbour,
            ),
        )[n]
        return pltpu.make_async_remote_copy(
            src_ref=source, dst_ref=target, send_sem=hop_send.at[n, p], recv_sem=hop_recv.at[n, p],
            device_id=device, device_id_type=MESH,
        )

    def dispatch(i):
        relayed = (odd == 1) & (i == relay_unit)

        @pl.when((i < 12) & jnp.logical_not(relayed))
        def _():
            send(i).start()

        @pl.when(relayed)
        def _():
            send(i, KEPT).start()
            for p in range(PIECES):
                hop(0, p).start()

        @pl.when(i >= 12)
        def _():
            keep(i).start()

    def block(b, carry):
        i = 2 * b
        g = place(i)[0]

        @pl.when(odd == 0)
        def _():
            rim_step(b)

        @pl.when((b == RELAY_BLOCK) & (odd == 0))
        def _():
            for p in range(PIECES):
                hop(0, p).wait_recv()
                hop(1, p).start()

        @pl.when((b == 0) | (b == 2))
        def _():
            ready(b // 2, 0)

        @pl.when(b == 0)
        def _():
            load_docs.wait()
            load_q(0).wait()

        @pl.when(b == 1)
        def _():
            load_q(1).wait()

        @pl.when(b == 4)
        def _():
            load_q(2).wait()

        parts = []
        for u in range(2):
            t = place(i + u)[1]
            reaches_back = jnp.where(t == 7, 0, odd)
            first = 3 - 3 * reaches_back
            count = (7 + t) // 2 + 1 - first
            begin = (docs[t] - 8 * tok + 7) * TILE
            doc_bias[u : u + 1, :] = jnp.where(
                lax.broadcasted_iota(jnp.int32, (1, doc_bias.shape[1]), 1) >= begin, 0.0, HIDDEN
            )
            key = lax.broadcasted_iota(jnp.int32, (TILE, CHUNK), 1) + (first + count - 1) * CHUNK
            row = lax.broadcasted_iota(jnp.int32, (TILE, CHUNK), 0) + (7 + t) * TILE
            last_bias[u] = jnp.where((key >= begin) & (key <= row), 0.0, HIDDEN)
            parts.append((t, first, count))

        for counts in ((1, 2), (2, 3), (3, 4), (4, 5), (5, 6), (6, 7), (7, 5)):
            @pl.when(parts[0][2] == counts[0])
            def _(counts=counts):
                attend(i, g, [(t, first, n) for (t, first, _), n in zip(parts, counts)])

        dispatch(i + 1)

        return carry

    lax.fori_loop(0, 8, block, 0)

    @pl.when(odd == 0)
    def _():
        for p in range(PIECES):
            hop(1, p).wait_recv()
            hop(2, p).start()

    def finish(i, carry):
        relayed = (odd == 1) & (i == relay_unit)

        @pl.when(jnp.logical_not(relayed))
        def _():
            send(i).wait_send()

        @pl.when(relayed)
        def _():
            send(i, KEPT).wait_send()

        return carry

    lax.fori_loop(0, 12, finish, 0)
    for i in range(12, 16):
        keep(i).wait()

    def arrive(n, carry):
        other = (head + 1 + n // 4) % 4
        g, half = (n // 2) % 2, n % 2

        def arrival(rows):
            return pltpu.make_async_remote_copy(
                src_ref=stage.at[0, pl.ds(0, rows)],
                dst_ref=out.at[
                    pl.ds(pl.multiple_of(half * TILE, TILE), rows),
                    pl.ds(pl.multiple_of((other * 2 + g) * QPK * HEAD_DIM, QPK * HEAD_DIM), QPK * HEAD_DIM),
                ],
                send_sem=send_sem.at[0],
                recv_sem=recv_sem.at[other, g, half],
                device_id=sibling,
                device_id_type=MESH,
            )

        relayed = (odd == 1) & (n == 5)

        @pl.when(jnp.logical_not(relayed))
        def _():
            arrival(TILE).wait_recv()

        @pl.when(relayed)
        def _():
            arrival(KEPT).wait_recv()

        return carry

    lax.fori_loop(0, 12, arrive, 0)

    @pl.when(odd == 0)
    def _():
        for p in range(PIECES):
            hop(1, p).wait_send()
            hop(2, p).wait_send()

    @pl.when(odd == 1)
    def _():
        for p in range(PIECES):
            hop(0, p).wait_send()
            hop(2, p).wait_recv()


def local(queries, keys, values, tile_docs):
    rows, width = queries.shape
    kv_width = keys.shape[1]
    groups = kv_width // HEAD_DIM
    heads = lax.axis_size("head")
    flops = 2 * 2 * 60 * TILE * TILE * width
    return pl.pallas_call(
        kernel,
        out_shape=pltpu.VMEM((rows // heads, width * heads), jnp.bfloat16),
        in_specs=[pl.BlockSpec(memory_space=pltpu.HBM)] * 4,
        out_specs=pl.BlockSpec(memory_space=pl.ANY),
        scratch_shapes=[
            pltpu.SMEM(tile_docs.shape, jnp.int32),
            pltpu.VMEM((rows, width), jnp.bfloat16),
            pltpu.VMEM((groups, 2 * rows, HEAD_DIM), jnp.bfloat16),
            pltpu.VMEM((groups, 2 * rows, HEAD_DIM), jnp.bfloat16),
            pltpu.VMEM((8, 2 * rows), jnp.float32),
            pltpu.VMEM((2, TILE, CHUNK), jnp.float32),
            pltpu.VMEM((16, TILE, QPK * HEAD_DIM), jnp.bfloat16),
            pltpu.SemaphoreType.DMA,
            pltpu.SemaphoreType.DMA((3,)),
            pltpu.SemaphoreType.DMA((2, 2)),
            pltpu.SemaphoreType.DMA((2, 2)),
            pltpu.SemaphoreType.DMA((2, 2)),
            pltpu.SemaphoreType.REGULAR,
            pltpu.SemaphoreType.DMA((12,)),
            pltpu.SemaphoreType.DMA((4, 2, 2)),
            pltpu.SemaphoreType.DMA((4,)),
            pltpu.VMEM((TILE, QPK * HEAD_DIM), jnp.bfloat16),
            pltpu.VMEM((TILE, QPK * HEAD_DIM), jnp.bfloat16),
            pltpu.SemaphoreType.DMA((3, PIECES)),
            pltpu.SemaphoreType.DMA((3, PIECES)),
        ],
        compiler_params=pltpu.CompilerParams(
            collective_id=0, has_side_effects=True, vmem_limit_bytes=59 << 20
        ),
        cost_estimate=pl.CostEstimate(
            flops=flops, bytes_accessed=10 << 20, transcendentals=60 * TILE * width
        ),
    )(tile_docs, queries, keys, values)


def solution(mesh):
    in_specs = (P("tok", "head"), P("tok", "head"), P("tok", "head"), P("tok"))
    out_specs = P(("tok", "head"), None)
    return jax.shard_map(local, mesh=mesh, in_specs=in_specs, out_specs=out_specs, check_vma=False)
```
